32 devices in a mesh: grp: 2 (over y), chan: 4 (over z), tm: 2 (over x), blk: 2 (over core).
Axes of the slice: x: 2, y: 2, z: 4, core: 2. Of those that a mesh axis runs over, the one named last changes fastest.
Arguments:
- samples: bfloat16 [32, 2048, 2048], P('tm', ('grp', 'chan', 'blk')), parts along dimension 1, may hold values from -6 to 6
- channel_gains: float32 [2, 1024, 1024], P(None, None, ('chan', 'blk')), may hold values from -4 to 4
- block_pairs: int32 [4, 2], P('blk'), may hold values from 0 to 7, as said below
Outputs:
- visibilities: float32 [2, 2048, 4, 128, 128], P(None, ('grp', 'chan', 'tm'), 'blk'), parts along dimension 1
The draws below stay inside these ranges and needn't reach their ends.
There are 2 independent parts, one for each index of `grp`. The reference program is written for one: setup_inputs(seed, part) draws one part's arguments, and reference() takes and returns one part's arrays. A program takes and returns all parts, laid end to end along the dimension named above; an argument that names none is the same for every part. Nothing has to cross between parts.
Inputs may be any that keep to these rules, and one draw needn't show every extreme that they name: `block_pairs`: each row holds two different input blocks, the smaller first; each of the 8 blocks appears in exactly one row.
All inputs are finite; a program needn't handle non-finite values.
Results may differ from the reference program's by a relative error of at most 0.0071.
Values may be sent and summed in bfloat16 or wider, within the bound.
A program may use at most 192 MiB of HBM per device.

```python
import math
import jax
import jax.numpy as jnp
from jax import lax

FRAME = 2048
NCH = 1024
TAPS = 16
NI = 1024
BLOCK = 128
NBLK = 8
SPECTRA = 32
PAIRS = 4


def draw_block_pairs(key, part):
    key = jax.random.fold_in(key, 11)
    shuffled = jax.random.permutation(key, NBLK).astype(jnp.int32).reshape(PAIRS, 2)
    return jnp.stack([jnp.min(shuffled, 1), jnp.max(shuffled, 1)], 1).astype(jnp.int32)


def block_levels(stream_key, extent, shards, low, largest):
    loudness = 1.0
    for dim, shards_of in shards:
        draws = jax.random.uniform(jax.random.fold_in(jax.random.fold_in(stream_key, 6), dim), (shards_of,), jnp.float32, low / len(shards), largest / len(shards))
        loudness = loudness * jnp.repeat(jnp.exp(draws), extent[dim] // shards_of).reshape((-1,) + (1,) * (len(extent) - 1 - dim))
    return loudness


def scatter_about(own_key, extent, deviation, bound, cuts=(), kind=jnp.bfloat16):
    array = deviation * jax.random.normal(own_key, extent, jnp.float32)
    if cuts:
        array = array * block_levels(own_key, extent, cuts, -0.22, 0.18)
    return jnp.clip(array, -bound, bound).astype(kind)


def setup_inputs(seed: int = 0, part: int = 0) -> dict:
    seeds = jax.random.split(jax.random.key(seed), 4)
    part_keys = jax.random.split(jax.random.fold_in(seeds[3], part), 4)
    samples = scatter_about(part_keys[0], (SPECTRA, NI, FRAME), 1.0, 6.0, ((0, 2), (1, 8)))
    channel_gains = scatter_about(seeds[1], (2, NCH, NI), 1.0, 4.0, ((2, 8),), jnp.float32)
    block_pairs = draw_block_pairs(jax.random.fold_in(seeds[3], 71), part)
    return {"samples": samples, "channel_gains": channel_gains, "block_pairs": block_pairs}


def filter_window(tap_count, frame_len):
    position = jnp.arange(tap_count * frame_len, dtype=jnp.int32).astype(jnp.float32)
    offset = (position + 0.5) / frame_len - tap_count / 2.0
    prototype = jnp.sin(jnp.pi * offset) / (jnp.pi * offset)
    prototype = prototype * (0.5 - 0.5 * jnp.cos(2.0 * jnp.pi * (position + 0.5) / (tap_count * frame_len)))
    return prototype.reshape(tap_count, frame_len)[::-1]

def channel_table(frame_len, chan_count):
    sample_idx = jnp.arange(frame_len, dtype=jnp.int32)[:, None]
    chan_idx = jnp.arange(chan_count, dtype=jnp.int32)[None, :]
    phase_angle = (sample_idx * chan_idx % frame_len).astype(jnp.float32) * (2.0 * math.pi / frame_len)
    norm_scale = 1.0 / math.sqrt(frame_len)
    return jnp.concatenate([jnp.cos(phase_angle) * norm_scale, -jnp.sin(phase_angle) * norm_scale], 1).astype(jnp.bfloat16)

def reference(samples, channel_gains, block_pairs):
    window = filter_window(TAPS, FRAME)
    dft_table = channel_table(FRAME, NCH)

    def block_volts(first_input):
        block_samples = lax.dynamic_slice_in_dim(samples, first_input, BLOCK, 1).astype(jnp.float32)
        padded = jnp.concatenate([jnp.zeros((TAPS - 1, BLOCK, FRAME), jnp.float32), block_samples], 0)
        filtered = jnp.zeros((SPECTRA, BLOCK, FRAME), jnp.float32)
        for tap in range(TAPS):
            filtered = filtered + window[tap] * padded[TAPS - 1 - tap:TAPS - 1 - tap + SPECTRA]
        filtered = filtered.astype(jnp.bfloat16).reshape(SPECTRA * BLOCK, FRAME)
        spectrum = jnp.dot(filtered, dft_table, preferred_element_type=jnp.float32).reshape(SPECTRA, BLOCK, 2, NCH)
        block_gains = lax.dynamic_slice_in_dim(channel_gains, first_input, BLOCK, 2)
        gain_real = jnp.transpose(block_gains[0])
        gain_imag = jnp.transpose(block_gains[1])
        spec_real = spectrum[:, :, 0]
        spec_imag = spectrum[:, :, 1]
        out_real = spec_real * gain_real - spec_imag * gain_imag
        out_imag = spec_real * gain_imag + spec_imag * gain_real
        return jnp.stack([out_real, out_imag], 2).astype(jnp.bfloat16)
    starts = jnp.arange(NBLK, dtype=jnp.int32) * BLOCK
    all_volts = lax.map(block_volts, starts)

    def pair_gram(pair_row):
        first_volts = all_volts[pair_row[0]].astype(jnp.float32)
        second_volts = all_volts[pair_row[1]].astype(jnp.float32)
        real_part = jnp.einsum('tprc,tqrc->cpq', first_volts, second_volts)
        turned = jnp.stack([first_volts[:, :, 1], -first_volts[:, :, 0]], 2)
        imag_part = jnp.einsum('tprc,tqrc->cpq', turned, second_volts)
        return jnp.stack([real_part, imag_part], 0)
    gram_stack = lax.map(pair_gram, block_pairs)
    return jnp.transpose(gram_stack, (1, 2, 0, 3, 4)) * (1.0 / math.sqrt(SPECTRA))
```

```python
import functools
import math

import jax
import jax.numpy as jnp
import ml_dtypes
import numpy as np
from jax import lax
from jax.experimental import pallas as pl
from jax.experimental.pallas import tpu as pltpu
from jax.sharding import PartitionSpec as P

NCH = 1024
TAPS = 16
BLOCK = 128


def passed_along(block, axis, distance):
    devices = range(lax.axis_size(axis))
    route = [(i - distance, i) for i in devices if i - distance in devices]
    return lax.ppermute(block, axis, route)


def filter_window(tap_count, frame_len):
    position = jnp.arange(tap_count * frame_len, dtype=jnp.int32).astype(jnp.float32)
    offset = (position + 0.5) / frame_len - tap_count / 2.0
    prototype = jnp.sin(jnp.pi * offset) / (jnp.pi * offset)
    prototype = prototype * (
        0.5 - 0.5 * jnp.cos(2.0 * jnp.pi * (position + 0.5) / (tap_count * frame_len))
    )
    return prototype.reshape(tap_count, frame_len)[::-1]


def channel_table(frame_len, chan_count):
    chan_idx = jnp.arange(chan_count, dtype=jnp.int32)[:, None]
    sample_idx = jnp.arange(frame_len, dtype=jnp.int32)[None, :]
    phase_angle = (sample_idx * chan_idx % frame_len).astype(jnp.float32) * (
        2.0 * math.pi / frame_len
    )
    norm_scale = 1.0 / math.sqrt(frame_len)
    return jnp.concatenate(
        [jnp.cos(phase_angle) * norm_scale, -jnp.sin(phase_angle) * norm_scale], 0
    ).astype(jnp.bfloat16)


def shards(samples, channel_gains, block_pairs):
    spectra_dev, inputs_dev, frame_len = samples.shape
    rim_frames = passed_along(samples[spectra_dev - (TAPS - 1) :], "tm", 1)
    padded = jnp.concatenate([rim_frames, samples], 0)
    window = filter_window(TAPS, frame_len)
    filtered = jnp.zeros((spectra_dev, inputs_dev, frame_len), jnp.float32)
    for tap in range(TAPS):
        filtered = filtered + window[tap] * padded[
            TAPS - 1 - tap : TAPS - 1 - tap + spectra_dev
        ].astype(jnp.float32)
    filtered = filtered.astype(jnp.bfloat16).reshape(spectra_dev * inputs_dev, frame_len)
    dft_table = channel_table(frame_len, NCH)
    spectrum = lax.dot_general(
        dft_table, filtered, (((1,), (1,)), ((), ())), preferred_element_type=jnp.float32
    )
    spectrum = spectrum.reshape(2, NCH, spectra_dev, inputs_dev)
    gain_real = channel_gains[0][:, None, :]
    gain_imag = channel_gains[1][:, None, :]
    volts = jnp.stack(
        [
            spectrum[0] * gain_real - spectrum[1] * gain_imag,
            spectrum[0] * gain_imag + spectrum[1] * gain_real,
        ],
        0,
    ).astype(jnp.bfloat16)
    n_chan = lax.axis_size("chan")
    n_time = lax.axis_size("tm")
    moved_parts = lax.all_to_all(
        volts[None], ("chan", "tm"), split_axis=2, concat_axis=0, tiled=True
    )
    chans_dev = moved_parts.shape[2]
    moved_parts = moved_parts.reshape(n_chan, n_time, 2, chans_dev, spectra_dev, inputs_dev)
    slab_volts = jnp.transpose(moved_parts, (2, 3, 1, 4, 0, 5)).reshape(
        2, chans_dev, n_time * spectra_dev, n_chan * inputs_dev
    )
    chans_dev = slab_volts.shape[1]
    time_count = slab_volts.shape[2]
    halves = lax.all_gather(slab_volts[:, :, :, None, :], "blk", axis=3, tiled=True)
    n_halves = halves.shape[3]
    all_inputs = halves.reshape(2, chans_dev, time_count, n_halves, n_chan, inputs_dev)
    all_inputs = jnp.transpose(all_inputs, (0, 1, 2, 4, 3, 5)).reshape(
        2, chans_dev, time_count, n_halves * n_chan * inputs_dev
    )
    norm_scale = 1.0 / math.sqrt(time_count)
    results = []
    for pair_slot in range(block_pairs.shape[0]):
        first_block = lax.dynamic_slice_in_dim(
            all_inputs, block_pairs[pair_slot, 0] * BLOCK, BLOCK, 3
        )
        second_block = lax.dynamic_slice_in_dim(
            all_inputs, block_pairs[pair_slot, 1] * BLOCK, BLOCK, 3
        )
        real_part = jnp.einsum(
            "rctp,rctq->cpq", first_block, second_block, preferred_element_type=jnp.float32
        )
        turned = jnp.stack([first_block[1], -first_block[0]], 0)
        imag_part = jnp.einsum(
            "rctp,rctq->cpq", turned, second_block, preferred_element_type=jnp.float32
        )
        results.append(jnp.stack([real_part, imag_part], 0) * norm_scale)
    return jnp.stack(results, 2)


CHUNK = 8
ROWS = 2 * CHUNK


def window_rows(tap_count, frame_len):
    offset = (np.arange(tap_count * frame_len) + 0.5) / frame_len - tap_count / 2.0
    taper = 0.5 - 0.5 * np.cos(2.0 * np.pi * (offset + tap_count / 2.0) / tap_count)
    rows = (np.sinc(offset) * taper).reshape(tap_count, frame_len)[::-1]
    return np.ascontiguousarray(
        np.broadcast_to(rows[:, None, :], (tap_count, 8, frame_len)).astype(np.float32)
    )


def table_rows(frame_len, chan_count):
    turn = np.arange(chan_count)[:, None] * np.arange(frame_len)[None, :] % frame_len
    angle = np.arange(frame_len) * (2.0 * np.pi / frame_len)
    scale = 1.0 / math.sqrt(frame_len)
    parts = np.stack([(np.cos(angle) * scale)[turn], (-np.sin(angle) * scale)[turn]], 0)
    return parts.astype(ml_dtypes.bfloat16)


def voltage_kernel(first, place_ref, x_ref, w_ref, tab_ref, gain_ref, other_ref, own_ref, filt, turned):
    step = pl.program_id(0)
    spectra, inputs, frame_len = x_ref.shape

    @pl.when(step == 0)
    def _():
        def tile(idx, carry):
            row = pl.multiple_of(idx // (frame_len // 128) * 16, 16)
            col = pl.multiple_of(idx % (frame_len // 128) * 128, 128)
            lo = max(0, first - TAPS + 1)
            hi = min(spectra, first + CHUNK)
            held = {
                s: x_ref[s, pl.ds(row, 16), pl.ds(col, 128)].astype(jnp.float32).reshape(2, 8, 128)
                for s in range(lo, hi)
            }
            sums = [None] * CHUNK
            for tap in range(TAPS):
                weight = w_ref[tap, :, pl.ds(col, 128)]
                for out in range(CHUNK):
                    s = first + out - tap
                    if lo <= s < hi:
                        term = held[s] * weight
                        sums[out] = term if sums[out] is None else sums[out] + term
            for out in range(CHUNK):
                total = sums[out]
                if total is None:
                    total = jnp.zeros((2, 8, 128), jnp.float32)
                filt[pl.ds(pl.multiple_of(out * inputs + row, 16), 16), pl.ds(col, 128)] = (
                    total.reshape(16, 128).astype(jnp.bfloat16)
                )
            return carry

        lax.fori_loop(0, inputs // 16 * (frame_len // 128), tile, 0)

    chans = tab_ref.shape[1]
    both = lax.dot_general(
        tab_ref[...].reshape(2 * chans, frame_len),
        filt[...],
        (((1,), (1,)), ((), ())),
        preferred_element_type=jnp.float32,
    )
    for s in range(CHUNK):
        real = both[:chans, s * inputs : (s + 1) * inputs]
        imag = both[chans:, s * inputs : (s + 1) * inputs]
        turned[s * chans : (s + 1) * chans, :] = real * gain_ref[0] - imag * gain_ref[1]
        turned[(CHUNK + s) * chans : (CHUNK + s + 1) * chans, :] = real * gain_ref[1] + imag * gain_ref[0]

    def write(out_ref):
        def one(chan, carry):
            out_ref[0, chan] = turned[pl.ds(chan, ROWS, stride=chans), :].astype(jnp.bfloat16)
            return carry

        lax.fori_loop(0, chans, one, 0, unroll=8)

    half = pl.num_programs(0) // 2

    @pl.when(step < half)
    def _():
        write(other_ref)

    @pl.when(step >= half)
    def _():
        write(own_ref)


def voltage_chunk(place, samples, window, table, gains, first):
    spectra, inputs, frame_len = samples.shape
    slabs = 4
    chans = table.shape[1] // (2 * slabs)

    def slab(step, place_ref):
        part = place_ref[1] ^ (1 - step // slabs)
        return (place_ref[0] ^ (step % slabs)) * 2 + part

    out = jax.ShapeDtypeStruct((slabs, chans, ROWS, inputs), jnp.bfloat16)
    flops = 2 * table.shape[1] * 2 * frame_len * CHUNK * inputs
    return pl.pallas_call(
        functools.partial(voltage_kernel, first),
        grid_spec=pltpu.PrefetchScalarGridSpec(
            num_scalar_prefetch=1,
            grid=(2 * slabs,),
            in_specs=[
                pl.BlockSpec((spectra, inputs, frame_len), lambda g, p: (0, 0, 0), pipeline_mode=pl.Buffered(1)),
                pl.BlockSpec((TAPS, 8, frame_len), lambda g, p: (0, 0, 0), pipeline_mode=pl.Buffered(1)),
                pl.BlockSpec((2, chans, frame_len), lambda g, p: (0, slab(g, p), 0)),
                pl.BlockSpec((2, chans, inputs), lambda g, p: (0, slab(g, p), 0)),
            ],
            out_specs=[
                pl.BlockSpec((1, chans, ROWS, inputs), lambda g, p: (jnp.minimum(g, slabs - 1), 0, 0, 0)),
                pl.BlockSpec((1, chans, ROWS, inputs), lambda g, p: (jnp.maximum(g - slabs, 0), 0, 0, 0)),
            ],
            scratch_shapes=[
                pltpu.VMEM((CHUNK * inputs, frame_len), jnp.bfloat16),
                pltpu.VMEM((ROWS * chans, inputs), jnp.float32),
            ],
        ),
        out_shape=[out, out],
        compiler_params=pltpu.CompilerParams(vmem_limit_bytes=40 << 20),
        cost_estimate=pl.CostEstimate(flops=flops, bytes_accessed=24 << 20, transcendentals=0),
    )(place, samples, window, table, gains)


def pair_kernel(scale, parts, where_ref, *refs):
    out_ref = refs[-1]
    slot = pl.program_id(0)
    sides = []
    for side in range(2):
        near = where_ref[slot * 4 + side * 2 + 1] == 0
        mine = refs[side * 2 * parts : side * 2 * parts + parts]
        far = refs[side * 2 * parts + parts : (side + 1) * 2 * parts]
        sides.append((near, mine, far))

    def one(chan, carry):
        tiles = []
        for near, mine, far in sides:
            tiles.append(
                [jnp.where(near, m[0, chan], f[0, chan]).astype(jnp.float32) for m, f in zip(mine, far)]
            )
        first = jnp.concatenate(tiles[0], 0).astype(jnp.bfloat16)
        second = jnp.concatenate(tiles[1], 0).astype(jnp.bfloat16)
        swapped = jnp.concatenate(
            [piece for x in tiles[1] for piece in (-x[CHUNK:], x[:CHUNK])], 0
        ).astype(jnp.bfloat16)
        both = lax.dot_general(
            first,
            jnp.concatenate([second, swapped], 1),
            (((0,), (0,)), ((), ())),
            preferred_element_type=jnp.float32,
        ) * scale
        out_ref[0, chan, 0] = both[:, :BLOCK]
        out_ref[1, chan, 0] = both[:, BLOCK:]
        return carry

    lax.fori_loop(0, out_ref.shape[1], one, 0, unroll=4)


def pair_products(where, mine, far, slots, scale):
    blocks, chans, rows, inputs = mine[0].shape
    step = 16
    parts = len(mine)

    def spec(side):
        return pl.BlockSpec((1, step, rows, inputs), lambda m, c, w: (w[m * 4 + side * 2], c, 0, 0))

    return pl.pallas_call(
        functools.partial(pair_kernel, scale, parts),
        grid_spec=pltpu.PrefetchScalarGridSpec(
            num_scalar_prefetch=1,
            grid=(slots, chans // step),
            in_specs=[spec(0)] * (2 * parts) + [spec(1)] * (2 * parts),
            out_specs=pl.BlockSpec((2, step, 1, BLOCK, BLOCK), lambda m, c, w: (0, c, m, 0, 0)),
        ),
        out_shape=jax.ShapeDtypeStruct((2, chans, slots, BLOCK, BLOCK), jnp.float32),
        compiler_params=pltpu.CompilerParams(vmem_limit_bytes=40 << 20),
        cost_estimate=pl.CostEstimate(flops=4 << 30, bytes_accessed=50 << 20, transcendentals=0),
    )(where, *mine, *far, *mine, *far)


def quick_shards(samples, channel_gains, block_pairs):
    spectra = samples.shape[0]
    chan, part, half = lax.axis_index("chan"), lax.axis_index("tm"), lax.axis_index("blk")
    place = jnp.stack([chan, part]).astype(jnp.int32)
    window = jnp.asarray(window_rows(TAPS, samples.shape[2]))
    table = jnp.asarray(table_rows(samples.shape[2], NCH))
    early = part == 0

    def made(first):
        return voltage_chunk(place, samples, window, table, channel_gains, first)

    def across(block):
        return lax.ppermute(block, "tm", [(0, 1), (1, 0)])

    def spread(pieces):
        moved = [pieces[0]]
        for d in range(1, 4):
            moved.append(lax.ppermute(pieces[d], "chan", [(i, i ^ d) for i in range(4)]))
        mine = jnp.stack(moved, 0)
        return mine, lax.ppermute(mine, "blk", [(0, 1), (1, 0)])

    def added(a, b):
        return (a.astype(jnp.float32) + b.astype(jnp.float32)).astype(jnp.bfloat16)

    mine, far = [], []
    for chunk in range(spectra // CHUNK):
        other, own = made(chunk * CHUNK)
        got = across(other)
        other_tail, own_tail = made(spectra + chunk * CHUNK)
        got_tail = lax.ppermute(other_tail, "tm", [(0, 1)])
        for pieces in (
            [jnp.where(early, own[d], got[d]) for d in range(4)],
            [
                jnp.where(early, added(got[d], own_tail[d]), added(own[d], got_tail[d]))
                for d in range(4)
            ],
        ):
            a, b = spread(pieces)
            mine.append(a)
            far.append(b)
    source = (block_pairs // 2) ^ chan
    elsewhere = (block_pairs % 2) ^ half
    where = jnp.stack([source, elsewhere], 2).reshape(-1).astype(jnp.int32)
    return pair_products(where, mine, far, block_pairs.shape[0], 1.0 / math.sqrt(2 * spectra))


def solution(mesh):
    sizes = dict(mesh.shape)
    quick = sizes["chan"] == 4 and sizes["tm"] == 2 and sizes["blk"] == 2
    placed = (P("tm", ("grp", "chan", "blk"), None), P(None, None, ("chan", "blk")), P("blk", None))
    return jax.shard_map(
        quick_shards if quick else shards,
        mesh=mesh,
        in_specs=placed,
        out_specs=P(None, ("grp", "chan", "tm"), "blk", None, None),
        check_vma=False,
    )
```

```python
import functools
import math

import jax
import jax.numpy as jnp
import ml_dtypes
import numpy as np
from jax import lax
from jax.experimental import pallas as pl
from jax.experimental.pallas import tpu as pltpu
from jax.sharding import PartitionSpec as P

NCH = 1024
TAPS = 16
BLOCK = 128


def passed_along(block, axis, distance):
    devices = range(lax.axis_size(axis))
    route = [(i - distance, i) for i in devices if i - distance in devices]
    return lax.ppermute(block, axis, route)


def filter_window(tap_count, frame_len):
    position = jnp.arange(tap_count * frame_len, dtype=jnp.int32).astype(jnp.float32)
    offset = (position + 0.5) / frame_len - tap_count / 2.0
    prototype = jnp.sin(jnp.pi * offset) / (jnp.pi * offset)
    prototype = prototype * (
        0.5 - 0.5 * jnp.cos(2.0 * jnp.pi * (position + 0.5) / (tap_count * frame_len))
    )
    return prototype.reshape(tap_count, frame_len)[::-1]


def channel_table(frame_len, chan_count):
    chan_idx = jnp.arange(chan_count, dtype=jnp.int32)[:, None]
    sample_idx = jnp.arange(frame_len, dtype=jnp.int32)[None, :]
    phase_angle = (sample_idx * chan_idx % frame_len).astype(jnp.float32) * (
        2.0 * math.pi / frame_len
    )
    norm_scale = 1.0 / math.sqrt(frame_len)
    return jnp.concatenate(
        [jnp.cos(phase_angle) * norm_scale, -jnp.sin(phase_angle) * norm_scale], 0
    ).astype(jnp.bfloat16)


def shards(samples, channel_gains, block_pairs):
    spectra_dev, inputs_dev, frame_len = samples.shape
    rim_frames = passed_along(samples[spectra_dev - (TAPS - 1) :], "tm", 1)
    padded = jnp.concatenate([rim_frames, samples], 0)
    window = filter_window(TAPS, frame_len)
    filtered = jnp.zeros((spectra_dev, inputs_dev, frame_len), jnp.float32)
    for tap in range(TAPS):
        filtered = filtered + window[tap] * padded[
            TAPS - 1 - tap : TAPS - 1 - tap + spectra_dev
        ].astype(jnp.float32)
    filtered = filtered.astype(jnp.bfloat16).reshape(spectra_dev * inputs_dev, frame_len)
    dft_table = channel_table(frame_len, NCH)
    spectrum = lax.dot_general(
        dft_table, filtered, (((1,), (1,)), ((), ())), preferred_element_type=jnp.float32
    )
    spectrum = spectrum.reshape(2, NCH, spectra_dev, inputs_dev)
    gain_real = channel_gains[0][:, None, :]
    gain_imag = channel_gains[1][:, None, :]
    volts = jnp.stack(
        [
            spectrum[0] * gain_real - spectrum[1] * gain_imag,
            spectrum[0] * gain_imag + spectrum[1] * gain_real,
        ],
        0,
    ).astype(jnp.bfloat16)
    n_chan = lax.axis_size("chan")
    n_time = lax.axis_size("tm")
    moved_parts = lax.all_to_all(
        volts[None], ("chan", "tm"), split_axis=2, concat_axis=0, tiled=True
    )
    chans_dev = moved_parts.shape[2]
    moved_parts = moved_parts.reshape(n_chan, n_time, 2, chans_dev, spectra_dev, inputs_dev)
    slab_volts = jnp.transpose(moved_parts, (2, 3, 1, 4, 0, 5)).reshape(
        2, chans_dev, n_time * spectra_dev, n_chan * inputs_dev
    )
    chans_dev = slab_volts.shape[1]
    time_count = slab_volts.shape[2]
    halves = lax.all_gather(slab_volts[:, :, :, None, :], "blk", axis=3, tiled=True)
    n_halves = halves.shape[3]
    all_inputs = halves.reshape(2, chans_dev, time_count, n_halves, n_chan, inputs_dev)
    all_inputs = jnp.transpose(all_inputs, (0, 1, 2, 4, 3, 5)).reshape(
        2, chans_dev, time_count, n_halves * n_chan * inputs_dev
    )
    norm_scale = 1.0 / math.sqrt(time_count)
    results = []
    for pair_slot in range(block_pairs.shape[0]):
        first_block = lax.dynamic_slice_in_dim(
            all_inputs, block_pairs[pair_slot, 0] * BLOCK, BLOCK, 3
        )
        second_block = lax.dynamic_slice_in_dim(
            all_inputs, block_pairs[pair_slot, 1] * BLOCK, BLOCK, 3
        )
        real_part = jnp.einsum(
            "rctp,rctq->cpq", first_block, second_block, preferred_element_type=jnp.float32
        )
        turned = jnp.stack([first_block[1], -first_block[0]], 0)
        imag_part = jnp.einsum(
            "rctp,rctq->cpq", turned, second_block, preferred_element_type=jnp.float32
        )
        results.append(jnp.stack([real_part, imag_part], 0) * norm_scale)
    return jnp.stack(results, 2)


CHUNK = 8
ROWS = 2 * CHUNK


def window_rows(tap_count, frame_len):
    offset = (np.arange(tap_count * frame_len) + 0.5) / frame_len - tap_count / 2.0
    taper = 0.5 - 0.5 * np.cos(2.0 * np.pi * (offset + tap_count / 2.0) / tap_count)
    rows = (np.sinc(offset) * taper).reshape(tap_count, frame_len)[::-1]
    return np.ascontiguousarray(
        np.broadcast_to(rows[:, None, :], (tap_count, 8, frame_len)).astype(np.float32)
    )


def table_rows(frame_len, chan_count):
    turn = np.arange(chan_count)[:, None] * np.arange(frame_len)[None, :] % frame_len
    angle = np.arange(frame_len) * (2.0 * np.pi / frame_len)
    scale = 1.0 / math.sqrt(frame_len)
    parts = np.stack([(np.cos(angle) * scale)[turn], (-np.sin(angle) * scale)[turn]], 0)
    return parts.astype(ml_dtypes.bfloat16)


def voltage_kernel(first, place_ref, x_ref, w_ref, tab_ref, gain_ref, *refs):
    filt, turned = refs[-2:]
    slabs = (len(refs) - 2) // 2
    step = pl.program_id(0)
    spectra, inputs, frame_len = x_ref.shape

    @pl.when(step == 0)
    def _():
        def tile(idx, carry):
            col = pl.multiple_of(idx * 128, 128)

            lo = max(0, first - TAPS + 1)
            hi = min(spectra, first + CHUNK)
            weights = {}
            rows = [[] for _ in range(CHUNK)]
            for row in range(0, inputs, 16):
                held = {
                    s: x_ref[s, pl.ds(row, 16), pl.ds(col, 128)].astype(jnp.float32).reshape(2, 8, 128)
                    for s in range(lo, hi)
                }
                sums = [None] * CHUNK
                for tap in range(TAPS):
                    if not any(lo <= first + out - tap < hi for out in range(CHUNK)):
                        continue
                    weight = w_ref[tap, :, pl.ds(col, 128)]
                    for out in range(CHUNK):
                        s = first + out - tap
                        if lo <= s < hi:
                            term = held[s] * weight
                            sums[out] = term if sums[out] is None else sums[out] + term
                for out in range(CHUNK):
                    total = sums[out]
                    if total is None:
                        total = jnp.zeros((2, 8, 128), jnp.float32)
                    rows[out].append(total.reshape(16, 128).astype(jnp.bfloat16))
            for out in range(CHUNK):
                filt[pl.ds(col, 128), out * inputs : (out + 1) * inputs] = jnp.concatenate(rows[out], 0).T
            return carry

        lax.fori_loop(0, frame_len // 128, tile, 0)

    both_chans = tab_ref.shape[1]
    chans = both_chans // 2
    width = filt.shape[1] // 4
    each = width // inputs
    for quarter in range(4):
        both = jnp.dot(
            tab_ref[...].reshape(2 * both_chans, frame_len),
            filt[:, quarter * width : (quarter + 1) * width],
            preferred_element_type=jnp.float32,
        )
        for k in range(each):
            s = quarter * each + k
            real = both[:both_chans, k * inputs : (k + 1) * inputs]
            imag = both[both_chans:, k * inputs : (k + 1) * inputs]
            low = s * PITCH
            turned[low : low + both_chans, :] = real * gain_ref[0] - imag * gain_ref[1]
            low = (CHUNK + s) * PITCH
            turned[low : low + both_chans, :] = real * gain_ref[1] + imag * gain_ref[0]

    part = place_ref[1]
    for slab in range(slabs):

        @pl.when(step == slab)
        def _():
            for out_ref, base in ((refs[slab], (1 - part) * chans), (refs[slabs + slab], part * chans)):

                def one(chan, carry):
                    out_ref[chan] = turned[pl.ds(base + chan, ROWS, stride=PITCH), :].astype(jnp.bfloat16)
                    return carry

                lax.fori_loop(0, chans, one, 0, unroll=16)


PITCH = 257


def voltage_chunk(place, samples, window, table, gains, first):
    spectra, inputs, frame_len = samples.shape
    slabs = 4
    both_chans = table.shape[1] // slabs
    out = jax.ShapeDtypeStruct((both_chans // 2, ROWS, inputs), jnp.bfloat16)
    flops = 2 * table.shape[1] * 2 * frame_len * CHUNK * inputs
    whole = pl.BlockSpec(out.shape, lambda g, p: (0, 0, 0))
    outs = pl.pallas_call(
        functools.partial(voltage_kernel, first),
        grid_spec=pltpu.PrefetchScalarGridSpec(
            num_scalar_prefetch=1,
            grid=(slabs,),
            in_specs=[
                pl.BlockSpec((spectra, inputs, frame_len), lambda g, p: (0, 0, 0), pipeline_mode=pl.Buffered(1)),
                pl.BlockSpec((TAPS, 8, frame_len), lambda g, p: (0, 0, 0), pipeline_mode=pl.Buffered(1)),
                pl.BlockSpec((2, both_chans, frame_len), lambda g, p: (0, p[0] ^ g, 0)),
                pl.BlockSpec((2, both_chans, inputs), lambda g, p: (0, p[0] ^ g, 0)),
            ],
            out_specs=[whole] * (2 * slabs),
            scratch_shapes=[
                pltpu.VMEM((frame_len, CHUNK * inputs), jnp.bfloat16),
                pltpu.VMEM((ROWS * PITCH, inputs), jnp.float32),
            ],
        ),
        out_shape=[out] * (2 * slabs),
        compiler_params=pltpu.CompilerParams(vmem_limit_bytes=48 << 20),
        cost_estimate=pl.CostEstimate(flops=flops, bytes_accessed=24 << 20, transcendentals=0),
    )(place, samples, window, table, gains)
    return outs[:slabs], outs[slabs:]


def pair_kernel(scale, parts, where_ref, *refs):
    out_ref = refs[-1]
    slot = pl.program_id(0)
    sides = []
    for side in range(2):
        near = where_ref[slot * 4 + side * 2 + 1] == 0
        mine = refs[side * 2 * parts : side * 2 * parts + parts]
        far = refs[side * 2 * parts + parts : (side + 1) * 2 * parts]
        sides.append((near, mine, far))

    def one(chan, carry):
        tiles = []
        for near, mine, far in sides:
            tiles.append(
                [jnp.where(near, m[0, chan], f[0, chan]) for m, f in zip(mine, far)]
            )
        first = jnp.concatenate(tiles[0], 0)
        second = jnp.concatenate(tiles[1], 0)
        swapped = jnp.concatenate(
            [
                piece
                for x in (tile.astype(jnp.float32) for tile in tiles[1])
                for piece in (-x[CHUNK:], x[:CHUNK])
            ],
            0,
        ).astype(jnp.bfloat16)
        both = lax.dot_general(
            first,
            jnp.concatenate([second, swapped], 1),
            (((0,), (0,)), ((), ())),
            preferred_element_type=jnp.float32,
        ) * scale
        out_ref[0, chan, 0] = both[:, :BLOCK]
        out_ref[1, chan, 0] = both[:, BLOCK:]
        return carry

    lax.fori_loop(0, out_ref.shape[1], one, 0, unroll=16)


def pair_products(where, mine, far, slots, scale):
    blocks, chans, rows, inputs = mine[0].shape
    step = 16
    parts = len(mine)

    def spec(side):
        return pl.BlockSpec((1, step, rows, inputs), lambda m, c, w: (w[m * 4 + side * 2], c, 0, 0))

    return pl.pallas_call(
        functools.partial(pair_kernel, scale, parts),
        grid_spec=pltpu.PrefetchScalarGridSpec(
            num_scalar_prefetch=1,
            grid=(slots, chans // step),
            in_specs=[spec(0)] * (2 * parts) + [spec(1)] * (2 * parts),
            out_specs=pl.BlockSpec((2, step, 1, BLOCK, BLOCK), lambda m, c, w: (0, c, m, 0, 0)),
        ),
        out_shape=jax.ShapeDtypeStruct((2, chans, slots, BLOCK, BLOCK), jnp.float32),
        compiler_params=pltpu.CompilerParams(vmem_limit_bytes=40 << 20),
        cost_estimate=pl.CostEstimate(flops=4 << 30, bytes_accessed=50 << 20, transcendentals=0),
    )(where, *mine, *far, *mine, *far)


def quick_shards(samples, channel_gains, block_pairs):
    spectra = samples.shape[0]
    chan, part, half = lax.axis_index("chan"), lax.axis_index("tm"), lax.axis_index("blk")
    place = jnp.stack([chan, part]).astype(jnp.int32)
    window = jnp.asarray(window_rows(TAPS, samples.shape[2]))
    table = jnp.asarray(table_rows(samples.shape[2], NCH))
    early = part == 0

    def made(first, after=()):
        block, *_ = lax.optimization_barrier((samples, *after))
        return voltage_chunk(place, block, window, table, channel_gains, first)

    def across(pieces, route):
        moved = [None] * 4
        for d in (3, 2, 1, 0):
            moved[d] = lax.ppermute(pieces[d], "tm", route)
        return moved

    def spread(pieces):
        moved = [pieces[0]]
        for d in range(1, 4):
            moved.append(lax.ppermute(pieces[d], "chan", [(i, i ^ d) for i in range(4)]))
        mine = jnp.stack(moved, 0)
        return mine, lax.ppermute(mine, "blk", [(0, 1), (1, 0)])

    def added(a, b):
        return (a.astype(jnp.float32) + b.astype(jnp.float32)).astype(jnp.bfloat16)

    mine, far = [], []
    ready = ()
    for chunk in range(spectra // CHUNK):
        other, own = made(chunk * CHUNK, ready)
        got = across(other, [(0, 1), (1, 0)])
        now = [jnp.where(early, own[d], got[d]) for d in range(4)]
        other_tail, own_tail = made(spectra + chunk * CHUNK, ready + (now[3],) if chunk == 0 else ready)
        got_tail = across(other_tail, [(0, 1)])
        ready = (now[2], now[1])
        later = [
            jnp.where(early, added(got[d], own_tail[d]), added(own[d], got_tail[d])) for d in range(4)
        ]
        for pieces in (now, later):
            a, b = spread(pieces)
            mine.append(a)
            far.append(b)
    source = (block_pairs // 2) ^ chan
    elsewhere = (block_pairs % 2) ^ half
    where = jnp.stack([source, elsewhere], 2).reshape(-1).astype(jnp.int32)
    return pair_products(where, mine, far, block_pairs.shape[0], 1.0 / math.sqrt(2 * spectra))


def solution(mesh):
    sizes = dict(mesh.shape)
    quick = sizes["chan"] == 4 and sizes["tm"] == 2 and sizes["blk"] == 2
    placed = (P("tm", ("grp", "chan", "blk"), None), P(None, None, ("chan", "blk")), P("blk", None))
    return jax.shard_map(
        quick_shards if quick else shards,
        mesh=mesh,
        in_specs=placed,
        out_specs=P(None, ("grp", "chan", "tm"), "blk", None, None),
        check_vma=False,
    )
```

```python
import functools
import math

import jax
import jax.numpy as jnp
import ml_dtypes
import numpy as np
from jax import lax
from jax.experimental import pallas as pl
from jax.experimental.pallas import tpu as pltpu
from jax.sharding import PartitionSpec as P

NCH = 1024
TAPS = 16
BLOCK = 128


def passed_along(block, axis, distance):
    devices = range(lax.axis_size(axis))
    route = [(i - distance, i) for i in devices if i - distance in devices]
    return lax.ppermute(block, axis, route)


def filter_window(tap_count, frame_len):
    position = jnp.arange(tap_count * frame_len, dtype=jnp.int32).astype(jnp.float32)
    offset = (position + 0.5) / frame_len - tap_count / 2.0
    prototype = jnp.sin(jnp.pi * offset) / (jnp.pi * offset)
    prototype = prototype * (
        0.5 - 0.5 * jnp.cos(2.0 * jnp.pi * (position + 0.5) / (tap_count * frame_len))
    )
    return prototype.reshape(tap_count, frame_len)[::-1]


def channel_table(frame_len, chan_count):
    chan_idx = jnp.arange(chan_count, dtype=jnp.int32)[:, None]
    sample_idx = jnp.arange(frame_len, dtype=jnp.int32)[None, :]
    phase_angle = (sample_idx * chan_idx % frame_len).astype(jnp.float32) * (
        2.0 * math.pi / frame_len
    )
    norm_scale = 1.0 / math.sqrt(frame_len)
    return jnp.concatenate(
        [jnp.cos(phase_angle) * norm_scale, -jnp.sin(phase_angle) * norm_scale], 0
    ).astype(jnp.bfloat16)


def shards(samples, channel_gains, block_pairs):
    spectra_dev, inputs_dev, frame_len = samples.shape
    rim_frames = passed_along(samples[spectra_dev - (TAPS - 1) :], "tm", 1)
    padded = jnp.concatenate([rim_frames, samples], 0)
    window = filter_window(TAPS, frame_len)
    filtered = jnp.zeros((spectra_dev, inputs_dev, frame_len), jnp.float32)
    for tap in range(TAPS):
        filtered = filtered + window[tap] * padded[
            TAPS - 1 - tap : TAPS - 1 - tap + spectra_dev
        ].astype(jnp.float32)
    filtered = filtered.astype(jnp.bfloat16).reshape(spectra_dev * inputs_dev, frame_len)
    dft_table = channel_table(frame_len, NCH)
    spectrum = lax.dot_general(
        dft_table, filtered, (((1,), (1,)), ((), ())), preferred_element_type=jnp.float32
    )
    spectrum = spectrum.reshape(2, NCH, spectra_dev, inputs_dev)
    gain_real = channel_gains[0][:, None, :]
    gain_imag = channel_gains[1][:, None, :]
    volts = jnp.stack(
        [
            spectrum[0] * gain_real - spectrum[1] * gain_imag,
            spectrum[0] * gain_imag + spectrum[1] * gain_real,
        ],
        0,
    ).astype(jnp.bfloat16)
    n_chan = lax.axis_size("chan")
    n_time = lax.axis_size("tm")
    moved_parts = lax.all_to_all(
        volts[None], ("chan", "tm"), split_axis=2, concat_axis=0, tiled=True
    )
    chans_dev = moved_parts.shape[2]
    moved_parts = moved_parts.reshape(n_chan, n_time, 2, chans_dev, spectra_dev, inputs_dev)
    slab_volts = jnp.transpose(moved_parts, (2, 3, 1, 4, 0, 5)).reshape(
        2, chans_dev, n_time * spectra_dev, n_chan * inputs_dev
    )
    chans_dev = slab_volts.shape[1]
    time_count = slab_volts.shape[2]
    halves = lax.all_gather(slab_volts[:, :, :, None, :], "blk", axis=3, tiled=True)
    n_halves = halves.shape[3]
    all_inputs = halves.reshape(2, chans_dev, time_count, n_halves, n_chan, inputs_dev)
    all_inputs = jnp.transpose(all_inputs, (0, 1, 2, 4, 3, 5)).reshape(
        2, chans_dev, time_count, n_halves * n_chan * inputs_dev
    )
    norm_scale = 1.0 / math.sqrt(time_count)
    results = []
    for pair_slot in range(block_pairs.shape[0]):
        first_block = lax.dynamic_slice_in_dim(
            all_inputs, block_pairs[pair_slot, 0] * BLOCK, BLOCK, 3
        )
        second_block = lax.dynamic_slice_in_dim(
            all_inputs, block_pairs[pair_slot, 1] * BLOCK, BLOCK, 3
        )
        real_part = jnp.einsum(
            "rctp,rctq->cpq", first_block, second_block, preferred_element_type=jnp.float32
        )
        turned = jnp.stack([first_block[1], -first_block[0]], 0)
        imag_part = jnp.einsum(
            "rctp,rctq->cpq", turned, second_block, preferred_element_type=jnp.float32
        )
        results.append(jnp.stack([real_part, imag_part], 0) * norm_scale)
    return jnp.stack(results, 2)


CHUNK = 8
ROWS = 2 * CHUNK


def window_rows(tap_count, frame_len):
    offset = (np.arange(tap_count * frame_len) + 0.5) / frame_len - tap_count / 2.0
    taper = 0.5 - 0.5 * np.cos(2.0 * np.pi * (offset + tap_count / 2.0) / tap_count)
    rows = (np.sinc(offset) * taper).reshape(tap_count, frame_len)[::-1]
    return np.ascontiguousarray(
        np.broadcast_to(rows[:, None, :], (tap_count, 8, frame_len)).astype(np.float32)
    )


def table_rows(frame_len, chan_count):
    turn = np.arange(chan_count)[:, None] * np.arange(frame_len)[None, :] % frame_len
    angle = np.arange(frame_len) * (2.0 * np.pi / frame_len)
    scale = 1.0 / math.sqrt(frame_len)
    parts = np.stack([(np.cos(angle) * scale)[turn], (-np.sin(angle) * scale)[turn]], 0)
    return parts.astype(ml_dtypes.bfloat16)


def voltage_kernel(first, cuts, place_ref, x_ref, w_ref, tab_ref, gain_ref, *refs):
    filt, turned = refs[-2:]
    slabs = 4
    others, owns = refs[:cuts], refs[cuts:-2]
    step = pl.program_id(0)
    spectra, inputs, frame_len = x_ref.shape

    @pl.when(step == 0)
    def _():
        def tile(idx, carry):
            col = pl.multiple_of(idx * 128, 128)

            lo = max(0, first - TAPS + 1)
            hi = min(spectra, first + CHUNK)
            weights = {}
            rows = [[] for _ in range(CHUNK)]
            for row in range(0, inputs, 16):
                held = {
                    s: x_ref[s, pl.ds(row, 16), pl.ds(col, 128)].astype(jnp.float32).reshape(2, 8, 128)
                    for s in range(lo, hi)
                }
                sums = [None] * CHUNK
                for tap in range(TAPS):
                    if not any(lo <= first + out - tap < hi for out in range(CHUNK)):
                        continue
                    weight = w_ref[tap, :, pl.ds(col, 128)]
                    for out in range(CHUNK):
                        s = first + out - tap
                        if lo <= s < hi:
                            term = held[s] * weight
                            sums[out] = term if sums[out] is None else sums[out] + term
                for out in range(CHUNK):
                    total = sums[out]
                    if total is None:
                        total = jnp.zeros((2, 8, 128), jnp.float32)
                    rows[out].append(total.reshape(16, 128).astype(jnp.bfloat16))
            for out in range(CHUNK):
                filt[pl.ds(col, 128), out * inputs : (out + 1) * inputs] = jnp.concatenate(rows[out], 0).T
            return carry

        lax.fori_loop(0, frame_len // 128, tile, 0)

    both_chans = tab_ref.shape[1]
    chans = both_chans // 2
    width = filt.shape[1] // 4
    each = width // inputs
    for quarter in range(4):
        both = jnp.dot(
            tab_ref[...].reshape(2 * both_chans, frame_len),
            filt[:, quarter * width : (quarter + 1) * width],
            preferred_element_type=jnp.float32,
        )
        for k in range(each):
            s = quarter * each + k
            real = both[:both_chans, k * inputs : (k + 1) * inputs]
            imag = both[both_chans:, k * inputs : (k + 1) * inputs]
            low = s * PITCH
            turned[low : low + both_chans, :] = real * gain_ref[0] - imag * gain_ref[1]
            low = (CHUNK + s) * PITCH
            turned[low : low + both_chans, :] = real * gain_ref[1] + imag * gain_ref[0]

    part = place_ref[1]
    for slab in range(slabs):

        @pl.when(step == slab)
        def _():
            sent = others[slab * cuts // slabs].at[slab % (slabs // cuts)]
            for out_ref, base in ((sent, (1 - part) * chans), (owns[slab], part * chans)):

                def one(chan, carry):
                    out_ref[chan] = turned[pl.ds(base + chan, ROWS, stride=PITCH), :].astype(jnp.bfloat16)
                    return carry

                lax.fori_loop(0, chans, one, 0, unroll=16)


PITCH = 257


def voltage_chunk(place, samples, window, table, gains, first, cuts):
    spectra, inputs, frame_len = samples.shape
    slabs = 4
    both_chans = table.shape[1] // slabs
    out = jax.ShapeDtypeStruct((both_chans // 2, ROWS, inputs), jnp.bfloat16)
    flops = 2 * table.shape[1] * 2 * frame_len * CHUNK * inputs
    whole = pl.BlockSpec(out.shape, lambda g, p: (0, 0, 0))
    twice = jax.ShapeDtypeStruct((slabs // cuts, *out.shape), jnp.bfloat16)
    pair = pl.BlockSpec(twice.shape, lambda g, p: (0, 0, 0, 0))
    outs = pl.pallas_call(
        functools.partial(voltage_kernel, first, cuts),
        grid_spec=pltpu.PrefetchScalarGridSpec(
            num_scalar_prefetch=1,
            grid=(slabs,),
            in_specs=[
                pl.BlockSpec((spectra, inputs, frame_len), lambda g, p: (0, 0, 0), pipeline_mode=pl.Buffered(1)),
                pl.BlockSpec((TAPS, 8, frame_len), lambda g, p: (0, 0, 0), pipeline_mode=pl.Buffered(1)),
                pl.BlockSpec((2, both_chans, frame_len), lambda g, p: (0, p[0] ^ (slabs - 1 - g), 0)),
                pl.BlockSpec((2, both_chans, inputs), lambda g, p: (0, p[0] ^ (slabs - 1 - g), 0)),
            ],
            out_specs=[pair] * cuts + [whole] * slabs,
            scratch_shapes=[
                pltpu.VMEM((frame_len, CHUNK * inputs), jnp.bfloat16),
                pltpu.VMEM((ROWS * PITCH, inputs), jnp.float32),
            ],
        ),
        out_shape=[twice] * cuts + [out] * slabs,
        compiler_params=pltpu.CompilerParams(vmem_limit_bytes=48 << 20),
        cost_estimate=pl.CostEstimate(flops=flops, bytes_accessed=24 << 20, transcendentals=0),
    )(place, samples, window, table, gains)
    return outs[:cuts], outs[cuts:][::-1]


def pair_kernel(scale, parts, where_ref, *refs):
    out_ref = refs[-1]
    slot = pl.program_id(0)
    sides = []
    for side in range(2):
        near = where_ref[slot * 4 + side * 2 + 1] == 0
        mine = refs[side * 2 * parts : side * 2 * parts + parts]
        far = refs[side * 2 * parts + parts : (side + 1) * 2 * parts]
        sides.append((near, mine, far))

    def one(chan, carry):
        tiles = []
        for near, mine, far in sides:
            tiles.append(
                [jnp.where(near, m[0, chan], f[0, chan]) for m, f in zip(mine, far)]
            )
        first = jnp.concatenate(tiles[0], 0)
        second = jnp.concatenate(tiles[1], 0)
        swapped = jnp.concatenate(
            [
                piece
                for x in (tile.astype(jnp.float32) for tile in tiles[1])
                for piece in (-x[CHUNK:], x[:CHUNK])
            ],
            0,
        ).astype(jnp.bfloat16)
        both = lax.dot_general(
            first,
            jnp.concatenate([second, swapped], 1),
            (((0,), (0,)), ((), ())),
            preferred_element_type=jnp.float32,
        ) * scale
        out_ref[0, chan, 0] = both[:, :BLOCK]
        out_ref[1, chan, 0] = both[:, BLOCK:]
        return carry

    lax.fori_loop(0, out_ref.shape[1], one, 0, unroll=16)


def pair_products(where, mine, far, slots, scale):
    blocks, chans, rows, inputs = mine[0].shape
    step = 16
    parts = len(mine)

    def spec(side):
        return pl.BlockSpec((1, step, rows, inputs), lambda m, c, w: (w[m * 4 + side * 2], c, 0, 0))

    return pl.pallas_call(
        functools.partial(pair_kernel, scale, parts),
        grid_spec=pltpu.PrefetchScalarGridSpec(
            num_scalar_prefetch=1,
            grid=(slots, chans // step),
            in_specs=[spec(0)] * (2 * parts) + [spec(1)] * (2 * parts),
            out_specs=pl.BlockSpec((2, step, 1, BLOCK, BLOCK), lambda m, c, w: (0, c, m, 0, 0)),
        ),
        out_shape=jax.ShapeDtypeStruct((2, chans, slots, BLOCK, BLOCK), jnp.float32),
        compiler_params=pltpu.CompilerParams(vmem_limit_bytes=40 << 20),
        cost_estimate=pl.CostEstimate(flops=4 << 30, bytes_accessed=50 << 20, transcendentals=0),
    )(where, *mine, *far, *mine, *far)


def quick_shards(samples, channel_gains, block_pairs):
    spectra = samples.shape[0]
    chan, part, half = lax.axis_index("chan"), lax.axis_index("tm"), lax.axis_index("blk")
    place = jnp.stack([chan, part]).astype(jnp.int32)
    window = jnp.asarray(window_rows(TAPS, samples.shape[2]))
    table = jnp.asarray(table_rows(samples.shape[2], NCH))
    early = part == 0

    def made(first, cuts, after=()):
        block, *_ = lax.optimization_barrier((samples, *after))
        return voltage_chunk(place, block, window, table, channel_gains, first, cuts)

    def across(pieces, route):
        got = [lax.ppermute(piece, "tm", route) for piece in pieces]
        return [piece[k] for piece in got for k in range(piece.shape[0])][::-1]

    def spread(pieces):
        moved = [pieces[0]]
        for d in (3, 2, 1):
            moved.insert(1, lax.ppermute(pieces[d], "chan", [(i, i ^ d) for i in range(4)]))
        return moved

    def twinned(moved):
        mine = jnp.stack(moved, 0)
        return mine, lax.ppermute(mine, "blk", [(0, 1), (1, 0)])

    def added(a, b):
        return (a.astype(jnp.float32) + b.astype(jnp.float32)).astype(jnp.bfloat16)

    both_ways, upward = [(0, 1), (1, 0)], [(0, 1)]
    chunks = spectra // CHUNK
    moved, after = [], ()
    for chunk in range(chunks):
        other, own = made(chunk * CHUNK, 2 if chunk == 0 else 1, after)
        got = across(other, both_ways)
        now = [jnp.where(early, own[d], got[d]) for d in range(4)]
        if chunk == 0:
            after = (own[0], now[3], now[2])
        else:
            after = (own[0], moved[0][2])
        other_tail, own_tail = made(spectra + chunk * CHUNK, 2 if chunk == chunks - 1 else 1, after)
        got_tail = across(other_tail, upward)
        moved.append(spread(now))
        after = (own_tail[0], now[1], moved[0][3])
        later = [
            jnp.where(early, added(got[d], own_tail[d]), added(own[d], got_tail[d])) for d in range(4)
        ]
        moved.append(spread(later))
    mine, far = zip(*[twinned(pieces) for pieces in moved])
    source = (block_pairs // 2) ^ chan
    elsewhere = (block_pairs % 2) ^ half
    where = jnp.stack([source, elsewhere], 2).reshape(-1).astype(jnp.int32)
    return pair_products(where, mine, far, block_pairs.shape[0], 1.0 / math.sqrt(2 * spectra))


def solution(mesh):
    sizes = dict(mesh.shape)
    quick = sizes["chan"] == 4 and sizes["tm"] == 2 and sizes["blk"] == 2
    placed = (P("tm", ("grp", "chan", "blk"), None), P(None, None, ("chan", "blk")), P("blk", None))
    return jax.shard_map(
        quick_shards if quick else shards,
        mesh=mesh,
        in_specs=placed,
        out_specs=P(None, ("grp", "chan", "tm"), "blk", None, None),
        check_vma=False,
    )
```
